512 devices in a mesh: row: 128 (over z, x, y_hi), gz: 4 (over y_lo, core).
Axes of the slice: x: 4, y: 4 (y_hi: 2, y_lo: 2; y = y_hi * 2 + y_lo), z: 16, core: 2. Of those that a mesh axis runs over, the one named last changes fastest.
Arguments:
- state: float32 [4, 1024, 16, 2048], P(None, 'row', 'gz'), may hold values from -12 to 12, as said below
- green: bfloat16 [128, 1024, 1024], P('row'), may hold values from -1 to 5
- vertical: float32 [16, 16], replicated, may hold values from 0 to 1
Outputs:
- new_state: float32 [4, 1024, 16, 2048], P(None, 'row', 'gz')
- potential: float32 [1024, 16, 2048], P('row', 'gz')
The draws below stay inside these ranges and needn't reach their ends.
Inputs may be any that keep to these rules, and one draw needn't show every extreme that they name: `state`: component 0 lies in 0.25 to 4; components 1 and 2 are at most 3 times component 0 in magnitude; component 3 lies between 0 and component 0.
All inputs are finite; a program needn't handle non-finite values.
Results may differ from the reference program's by a relative error of at most 0.0019.
Values may be sent and summed in bfloat16 or wider, within the bound.
A program may use at most 64 MiB of HBM per device.

```python
import math
import jax
import jax.numpy as jnp
from jax import lax

NR = 1024
NPHI = 2048
MODES = 128
ZW = 16


def draw_state(key, part):
    keys = jax.random.split(jax.random.fold_in(key, 11), 4)
    shape = (NR, ZW, NPHI)
    level = jax.random.uniform(keys[0], shape, jnp.float32)
    density = 0.5 * 4.0 ** level
    radial_speed = 0.5 * jnp.clip(jax.random.normal(keys[1], shape, jnp.float32), -3.0, 3.0)
    spin_speed = 1.0 + 0.5 * jnp.clip(jax.random.normal(keys[2], shape, jnp.float32), -3.0, 3.0)
    tracer = jax.random.uniform(keys[3], shape, jnp.float32)
    return jnp.stack([density, density * radial_speed, density * spin_speed, density * tracer]).astype(jnp.float32)


def draw_green(key, part):
    base = jax.random.fold_in(key, 23)
    index = jnp.arange(NR)
    distance = jnp.abs(index[:, None] - index[None, :]).astype(jnp.float32)
    reach = NR / 4.0

    def one_mode(mode):
        keys = jax.random.split(jax.random.fold_in(base, mode), 3)
        strength = 0.5 * 4.0 ** jax.random.uniform(keys[0], (), jnp.float32)
        smooth = jnp.exp(-distance / reach) * (4.0 / NR) * strength
        rough = 0.5 * jnp.clip(jax.random.normal(keys[1], (NR, NR), jnp.float32), -4.0, 4.0) / math.sqrt(NR)
        diagonal = 1.0 + jax.random.uniform(keys[2], (NR,), jnp.float32)
        return (jnp.diag(diagonal) + rough + smooth).astype(jnp.bfloat16)
    return lax.map(one_mode, jnp.arange(MODES))


def draw_vertical(key, part):
    width = ZW / 4.0
    index = jnp.arange(ZW).astype(jnp.float32)
    offset = index[:, None] - index[None, :]
    shape_factor = jnp.exp(-offset * offset / (2.0 * width * width)) / (width * math.sqrt(2.0 * math.pi))
    noise = jnp.clip(jax.random.normal(jax.random.fold_in(key, 37), (ZW, ZW), jnp.float32), -3.0, 3.0)
    return (shape_factor * (1.0 + 0.3 * noise)).astype(jnp.float32)


def setup_inputs(seed: int = 0) -> dict:
    seeds = jax.random.split(jax.random.key(seed), 4)
    return {
        "state": draw_state(jax.random.fold_in(seeds[3], 71), 0),
        "green": draw_green(jax.random.fold_in(seeds[3], 71), 0),
        "vertical": draw_vertical(jax.random.fold_in(seeds[3], 71), 0),
    }


sound_sq = 1.0
inner_radius = 1.0
radial_span = 4.0
courant = 0.2
precise = lax.Precision.HIGHEST

def mode_table(azimuth, modes):
    angle_index = jnp.arange(azimuth, dtype=jnp.int32)[:, None] * jnp.arange(modes, dtype=jnp.int32)[None, :] % azimuth
    angles = angle_index.astype(jnp.float32) * (2.0 * math.pi / azimuth)
    forward = jnp.concatenate([jnp.cos(angles), -jnp.sin(angles)], axis=1)
    weights = jnp.where(jnp.arange(modes) == 0, 1.0, 2.0) / azimuth
    weights = jnp.concatenate([weights, weights]).astype(jnp.float32)
    inverse = forward.T * weights[:, None]
    return (forward, inverse)

def minmod(former, latter):
    return jnp.where(former * latter > 0, jnp.where(jnp.abs(former) < jnp.abs(latter), former, latter), 0.0)

def rusanov(left_state, right_state, normal):
    onehot = (jnp.arange(4) == normal).astype(left_state.dtype).reshape(4, 1, 1, 1)

    def flux_of(values):
        velocity = values[normal] / values[0]
        return (values * velocity + sound_sq * values[0] * onehot, jnp.abs(velocity))
    flux_left, speed_left = flux_of(left_state)
    flux_right, speed_right = flux_of(right_state)
    reach = jnp.maximum(speed_left, speed_right) + math.sqrt(sound_sq)
    return 0.5 * (flux_left + flux_right) - 0.5 * reach * (right_state - left_state)

def advance(padded, potential, radial_slope, centres, radial_step):
    azimuth = padded.shape[-1]
    phi_step = 2.0 * math.pi / azimuth
    step_time = courant * min(radial_step, inner_radius * phi_step)
    slopes = minmod(padded[:, 1:-1] - padded[:, :-2], padded[:, 2:] - padded[:, 1:-1])
    centre_cells = padded[:, 1:-1]
    flux_radial = rusanov(centre_cells[:, :-1] + 0.5 * slopes[:, :-1], centre_cells[:, 1:] - 0.5 * slopes[:, 1:], 1)
    interior = padded[:, 2:-2]
    phi_slopes = minmod(interior - jnp.roll(interior, 1, axis=3), jnp.roll(interior, -1, axis=3) - interior)
    flux_phi = rusanov(interior + 0.5 * phi_slopes, jnp.roll(interior - 0.5 * phi_slopes, -1, axis=3), 2)
    face_radii = jnp.concatenate([centres - 0.5 * radial_step, centres[-1:] + 0.5 * radial_step]).reshape(1, -1, 1, 1)
    weighted = face_radii * flux_radial
    radius = centres.reshape(1, -1, 1, 1)
    tendency = -((weighted[:, 1:] - weighted[:, :-1]) / radial_step + (flux_phi - jnp.roll(flux_phi, 1, axis=3)) / phi_step) / radius
    density = interior[0]
    spin = interior[2] / density
    radius_cells = centres.reshape(-1, 1, 1)
    azimuth_slope = (jnp.roll(potential, -1, axis=2) - jnp.roll(potential, 1, axis=2)) / (2.0 * phi_step)
    force_radial = (interior[2] * spin + sound_sq * density) / radius_cells - density * radial_slope
    force_phi = -(interior[1] * spin + density * azimuth_slope) / radius_cells
    zeros = jnp.zeros_like(density)
    sources = jnp.stack([zeros, force_radial, force_phi, zeros])
    return interior + step_time * (tendency + sources)

def reference(state, green, vertical):
    forward, inverse = mode_table(NPHI, MODES)
    spectrum = jnp.dot(state[0].reshape(-1, NPHI), forward, precision=precise, preferred_element_type=jnp.float32).reshape(NR, ZW, 2, MODES)
    mixed = jnp.einsum('zy,ryck->rzck', vertical, spectrum, precision=precise)
    mixed_b = mixed.astype(jnp.bfloat16)

    def one_mode(operands):
        matrix, column = operands
        return jnp.einsum('rs,szc->rzc', matrix.astype(jnp.float32), column.astype(jnp.float32))
    mode_major = lax.map(one_mode, (green, jnp.moveaxis(mixed_b, 3, 0)))
    pot_spec = jnp.moveaxis(mode_major, 0, 3)
    potential = jnp.dot(pot_spec.reshape(-1, 2 * MODES), inverse, precision=precise, preferred_element_type=jnp.float32).reshape(NR, ZW, NPHI)
    radial_step = radial_span / NR
    padded_pot = jnp.pad(potential, ((1, 1), (0, 0), (0, 0)), mode='edge')
    radial_slope = (padded_pot[2:] - padded_pot[:-2]) / (2.0 * radial_step)
    padded = jnp.pad(state, ((0, 0), (2, 2), (0, 0), (0, 0)), mode='edge')
    centres = inner_radius + (jnp.arange(NR).astype(jnp.float32) + 0.5) * radial_step
    new_state = advance(padded, potential, radial_slope, centres, radial_step)
    return (new_state, potential)
```

```python
import functools
import math

import jax
import jax.numpy as jnp
import ml_dtypes
import numpy as np
from jax import lax
from jax.experimental import pallas as pl
from jax.experimental.pallas import tpu as pltpu
from jax.sharding import PartitionSpec as P

NR, NPHI, MODES, ZW = 1024, 2048, 128, 16
ROWS, GZ = 128, 4
DR = 4.0 / NR
DPHI = 2.0 * math.pi / NPHI
DT = 0.2 * min(DR, DPHI)
F32, BF16 = jnp.float32, jnp.bfloat16
MESH = pl.DeviceIdType.MESH
CHUNK = 256


def tables():
    index = np.arange(NPHI)[:, None] * np.arange(MODES)[None, :] % NPHI
    angles = 2.0 * np.pi * index / NPHI
    forward = np.concatenate([np.cos(angles), -np.sin(angles)], axis=1)
    weights = np.where(np.arange(MODES) == 0, 1.0, 2.0) / NPHI
    inverse = forward.T * np.concatenate([weights, weights])[:, None]
    out = []
    for table in (forward, inverse):
        high = table.astype(np.float32).astype(ml_dtypes.bfloat16)
        low = (table - high.astype(np.float64)).astype(np.float32).astype(ml_dtypes.bfloat16)
        out += [high, low]
    return out


def split(x):
    high = x.astype(BF16)
    return high, (x - high.astype(F32)).astype(BF16)


def dot(a, b):
    return jnp.dot(a, b, preferred_element_type=F32)


def iota(shape, dim):
    return lax.broadcasted_iota(jnp.int32, shape, dim)


def minmod_half(a, b):
    return jnp.where(a * b > 0, jnp.where(jnp.abs(a) < jnp.abs(b), a, b), 0.0) * 0.5


def rusanov(left, right, normal):
    v_left = left[normal] / left[0]
    v_right = right[normal] / right[0]
    reach = jnp.maximum(jnp.abs(v_left), jnp.abs(v_right)) + 1.0
    fluxes = []
    for k in range(4):
        both = left[k] * v_left + right[k] * v_right
        if k == normal:
            both = both + (left[0] + right[0])
        fluxes.append(0.5 * (both - reach * (right[k] - left[k])))
    return fluxes


def lanes(column, width):
    return jnp.concatenate([column] * (width // 128), axis=1)


def pair_row(shape):
    return (iota(shape, 0) >= 4).astype(jnp.int32)


def peer(row, k):
    step, low = k // 8, 7 - lax.rem(k, 8)
    half = (step + 1) // 2
    shift = jnp.where(lax.rem(step, 2) == 0, 8 + half, 8 - half)
    z, q = row // 8, lax.rem(row, 8)
    return lax.rem(z + shift, 16) * 8 + (q ^ low)


def exchange_kernel(
    state, green, vertical, t_high, t_low, part, spec,
    S, O, TH, TL, G, SA, msg, X, back, Y, LB, RB, FB, FR, acc,
    sem_in, sem_gs, sem_gr, sem_as, sem_ar, sem_bs, sem_br, sem_hs, sem_hr, sem_out,
):
    row, gz = lax.axis_index("row"), lax.axis_index("gz")

    def load_rows(fields, target, shift, sem):
        for r in range(8):
            t = r + 2 - shift
            pltpu.make_async_copy(
                state.at[fields, r], target.at[fields, t // 2, pl.ds(4 * (t % 2), 4)], sem
            ).start()

    load_rows(pl.ds(0, 1), S, 0, sem_in.at[0])
    load_t = [
        pltpu.make_async_copy(t_high, TH, sem_in.at[1]),
        pltpu.make_async_copy(t_low, TL, sem_in.at[2]),
    ]
    for copy in load_t:
        copy.start()
    load_rows(pl.ds(1, 3), S, 0, sem_in.at[3])
    load_rows(pl.ds(0, 4), O, 1, sem_in.at[4])
    load_g = pltpu.make_async_copy(green, G, sem_in.at[5])
    load_g.start()

    barrier = pltpu.get_barrier_semaphore()

    def greet(k, carry):
        pl.semaphore_signal(barrier, inc=1, device_id=(peer(row, k), gz), device_id_type=MESH)
        return carry

    lax.fori_loop(0, ROWS - 1, greet, 0)
    for k in range(1, GZ):
        pl.semaphore_signal(barrier, inc=1, device_id=(row, gz ^ k), device_id_type=MESH)

    pltpu.make_async_copy(S.at[0, pl.ds(1, 4)], S.at[0, pl.ds(1, 4)], sem_in.at[0]).wait()
    density = S[0, pl.ds(1, 4)].reshape(32, NPHI)
    high, low = split(density)
    load_t[0].wait()
    stacked = dot(jnp.concatenate([high, low], axis=0), TH[...])
    load_t[1].wait()
    own = pl.ds(pl.multiple_of(gz * 32, 32), 32)
    SA[own, :] = stacked[:32] + stacked[32:] + dot(high, TL[...])

    pl.semaphore_wait(barrier, ROWS - 1 + GZ - 1)
    gathers = []
    for k in range(1, GZ):
        gathers.append(
            pltpu.make_async_remote_copy(
                SA.at[own], SA.at[own], sem_gs.at[k], sem_gr.at[k],
                device_id=(row, gz ^ k), device_id_type=MESH,
            )
        )
        gathers[-1].start()

    a_row, a_col = iota((256, 16), 0), iota((256, 16), 1)
    pick_y = (a_col == 4 * ((a_row >> 5) & 3) + (a_row & 3)).astype(BF16)
    b_row, b_col = iota((16, 128), 0), iota((16, 128), 1)
    pick_z = (b_row == 4 * gz + (b_col & 3)).astype(BF16)
    w_row, w_col = iota((256, 128), 0), iota((256, 128), 1)
    w_keep = ((w_row >> 7) == (w_col >> 6)) & (((w_row >> 2) & 7) == ((w_col >> 2) & 15))
    weights = []
    for piece in split(vertical[...]):
        rows_y = lax.dot_general(
            pick_y, piece, (((1,), (1,)), ((), ())), preferred_element_type=F32
        ).astype(BF16)
        weights.append(jnp.where(w_keep, dot(rows_y, pick_z), 0.0).astype(BF16))
    for copy in gathers:
        copy.wait()
    turned = jnp.concatenate([SA[:, :MODES].T, SA[:, MODES:].T], axis=1)
    high, low = split(turned)
    mixed = dot(high, weights[0]) + dot(low, weights[0]) + dot(high, weights[1])
    msg[...] = mixed.astype(BF16).astype(F32)

    def send_forward(k, carry):
        d = peer(row, k)
        pltpu.make_async_remote_copy(
            msg.at[pl.ds(d, 1)], X.at[row], sem_as, sem_ar, device_id=(d, gz), device_id_type=MESH
        ).start()
        return carry

    lax.fori_loop(0, ROWS - 1, send_forward, 0)
    X[row] = msg[pl.ds(row, 1), :]

    pltpu.make_async_copy(
        S.at[pl.ds(1, 3), pl.ds(1, 4)], S.at[pl.ds(1, 3), pl.ds(1, 4)], sem_in.at[3]
    ).wait()
    pltpu.make_async_copy(O.at[:, pl.ds(0, 4)], O.at[:, pl.ds(0, 4)], sem_in.at[4]).wait()
    down = pltpu.make_async_remote_copy(
        S.at[:, 1], S.at[:, 5], sem_hs.at[0], sem_hr.at[0],
        device_id=(jnp.maximum(row - 1, 0), gz), device_id_type=MESH,
    )
    up = pltpu.make_async_remote_copy(
        S.at[:, 4], S.at[:, 0], sem_hs.at[1], sem_hr.at[1],
        device_id=(jnp.minimum(row + 1, ROWS - 1), gz), device_id_type=MESH,
    )

    @pl.when(row > 0)
    def _():
        down.start()

    @pl.when(row < ROWS - 1)
    def _():
        up.start()

    first = row * 8

    def azimuth(j, carry):
        centre = 1.0 + ((first + 2 * j + pair_row((8, 128))).astype(F32) + 0.5) * DR
        inverse_r = lanes(1.0 / centre, CHUNK)
        for k in range(4):
            u = S[k, j + 1]
            back_diff = u - pltpu.roll(u, 1, 1)
            slope = minmod_half(back_diff, pltpu.roll(back_diff, NPHI - 1, 1))
            LB[k] = u + slope
            RB[k] = pltpu.roll(u - slope, NPHI - 1, 1)

        for c in range(NPHI // CHUNK):
            at = pl.ds(c * CHUNK, CHUNK)
            fluxes = rusanov([LB[k, :, at] for k in range(4)], [RB[k, :, at] for k in range(4)], 2)
            for k in range(4):
                FB[k, :, at] = fluxes[k]

        for k in range(4):
            flux = FB[k]
            LB[k] = flux - pltpu.roll(flux, 1, 1)

        for c in range(NPHI // CHUNK):
            at = pl.ds(c * CHUNK, CHUNK)
            u = [S[k, j + 1, :, at] for k in range(4)]
            spin = u[2] / u[0]
            gain = [None, u[2] * spin + u[0], -(u[1] * spin), None]
            for k in range(4):
                change = LB[k, :, at] * (-1.0 / DPHI)
                if gain[k] is not None:
                    change = change + gain[k]
                acc[k, j, :, at] = u[k] + DT * inverse_r * change
        return carry

    lax.fori_loop(0, 4, azimuth, 0)

    def radial(j, c):
        at = pl.ds(pl.multiple_of(c * CHUNK, CHUNK), CHUNK)
        face = lanes(1.0 + (first + 2 * j + pair_row((8, 128))).astype(F32) * DR, CHUNK)
        left, right = [], []
        for k in range(4):
            a0, a1, a2, a3 = S[k, j, :, at], O[k, j, :, at], S[k, j + 1, :, at], O[k, j + 1, :, at]
            middle = a2 - a1
            left.append(a1 + minmod_half(a1 - a0, middle))
            right.append(a2 - minmod_half(middle, a3 - a2))
        fluxes = rusanov(left, right, 1)
        for k in range(4):
            FR[k, j, :, at] = face * fluxes[k]

    pieces = NPHI // CHUNK

    def inner(i, carry):
        radial(1 + i // pieces, lax.rem(i, pieces))
        return carry

    lax.fori_loop(0, 2 * pieces, inner, 0)

    pltpu.make_async_copy(X.at[pl.ds(0, ROWS - 1)], X.at[pl.ds(0, ROWS - 1)], sem_ar).wait()
    load_g.wait()
    sub, lane = iota((ROWS, 8, 128), 1), iota((ROWS, 8, 128), 2)
    group = (lane >> 2) & 15
    spread = jnp.where(group == sub, jnp.broadcast_to(X[...], (ROWS, 8, 128)), 0.0)
    f_row, f_col = iota((128, 128), 0), iota((128, 128), 1)
    fold = (((f_row >> 6) == (f_col >> 6)) & ((f_row & 3) == (f_col & 3))).astype(BF16)
    columns = dot(spread.reshape(NR, 128).astype(BF16), fold).astype(BF16)
    solved = dot(G[...], columns).reshape(ROWS, 8, 128)
    keep = (group == sub + 1) | ((group == 0) & (sub == 7)) | ((group == 9) & (sub == 0))
    rows = jnp.sum(jnp.where(keep, solved, 0.0), axis=1)
    f_group = (f_col >> 2) & 15
    back[...] = jnp.where(
        f_group == 0, pltpu.roll(rows, 1, 0),
        jnp.where(f_group == 9, pltpu.roll(rows, ROWS - 1, 0), rows),
    )

    def send_back(k, carry):
        d = peer(row, k)
        pltpu.make_async_remote_copy(
            back.at[pl.ds(d, 1)], Y.at[pl.ds(row, 1)], sem_bs, sem_br,
            device_id=(d, gz), device_id_type=MESH,
        ).start()
        return carry

    lax.fori_loop(0, ROWS - 1, send_back, 0)
    Y[pl.ds(row, 1), :] = back[pl.ds(row, 1), :]

    @pl.when(row > 0)
    def _():
        down.wait_send()
        up.wait_recv()

    @pl.when(row < ROWS - 1)
    def _():
        up.wait_send()
        down.wait_recv()

    @pl.when(row == 0)
    def _():
        for k in range(4):
            S[k, 0, pl.ds(0, 4)] = S[k, 1, pl.ds(0, 4)]
            S[k, 0, pl.ds(4, 4)] = S[k, 1, pl.ds(0, 4)]

    @pl.when(row == ROWS - 1)
    def _():
        for k in range(4):
            S[k, 5, pl.ds(0, 4)] = S[k, 4, pl.ds(4, 4)]
            S[k, 5, pl.ds(4, 4)] = S[k, 4, pl.ds(4, 4)]

    for k in range(4):
        O[k, 0, pl.ds(0, 4)] = S[k, 0, pl.ds(4, 4)]
        O[k, 4, pl.ds(4, 4)] = S[k, 5, pl.ds(0, 4)]
        O[k, 5, pl.ds(0, 4)] = S[k, 5, pl.ds(4, 4)]
        O[k, 5, pl.ds(4, 4)] = S[k, 5, pl.ds(4, 4)]

    def edges(i, carry):
        piece = lax.rem(i, pieces)
        which = i // pieces
        radial(jnp.where(which == 0, 0, which + 2), piece)
        return carry

    lax.fori_loop(0, 3 * pieces, edges, 0)

    def gather_radial(i, carry):
        j, c = i // pieces, lax.rem(i, pieces)
        at = pl.ds(pl.multiple_of(c * CHUNK, CHUNK), CHUNK)
        centre = 1.0 + ((first + 2 * j + pair_row((8, 128))).astype(F32) + 0.5) * DR
        scale = lanes((DT / DR) / centre, CHUNK)
        second = iota((8, CHUNK), 0) >= 4
        for k in range(4):
            low_face = FR[k, j, :, at]
            high_face = pltpu.roll(jnp.where(second, low_face, FR[k, j + 1, :, at]), 4, 0)
            acc[k, j, :, at] = acc[k, j, :, at] - scale * (high_face - low_face)
        return carry

    lax.fori_loop(0, 4 * pieces, gather_radial, 0)
    out_part = pltpu.make_async_copy(acc, part, sem_out.at[0])
    out_part.start()

    pltpu.make_async_copy(Y.at[pl.ds(0, ROWS - 1)], Y.at[pl.ds(0, ROWS - 1)], sem_br).wait()
    out_spec = pltpu.make_async_copy(Y, spec, sem_out.at[1])
    out_spec.start()
    pltpu.make_async_copy(X.at[pl.ds(0, ROWS - 1)], X.at[pl.ds(0, ROWS - 1)], sem_as).wait()
    pltpu.make_async_copy(Y.at[pl.ds(0, ROWS - 1)], Y.at[pl.ds(0, ROWS - 1)], sem_bs).wait()
    out_part.wait()
    out_spec.wait()


def finish_kernel(state, part, spec, t_high, t_low, new_state, potential, D, M, TH, TL, PT, OUT, sem):
    row = lax.axis_index("row")
    load_t = [
        pltpu.make_async_copy(t_high, TH, sem.at[0]),
        pltpu.make_async_copy(t_low, TL, sem.at[1]),
    ]
    for copy in load_t:
        copy.start()
    for r in range(8):
        pltpu.make_async_copy(
            state.at[0, r], D.at[r // 2, pl.ds(4 * (r % 2), 4)], sem.at[2]
        ).start()
    load_m = pltpu.make_async_copy(part.at[pl.ds(1, 2)], M, sem.at[3])
    load_m.start()
    plain = []
    for i, k in enumerate((0, 3)):
        for r in range(8):
            plain.append(
                pltpu.make_async_copy(
                    part.at[k, r // 2, pl.ds(4 * (r % 2), 4)], new_state.at[k, r], sem.at[4 + i]
                )
            )
            plain[-1].start()

    turned = spec[...].T
    pieces = []
    for c in range(2):
        base = 64 * c
        own = turned[base + 4 : base + 36]
        ext = turned[base : base + 40]
        before = jnp.where(row == 0, turned[base + 4 : base + 8], turned[base : base + 4])
        after = jnp.where(row == ROWS - 1, turned[base + 32 : base + 36], turned[base + 36 : base + 40])
        pieces.append(jnp.concatenate([own, before, ext[4:36], after], axis=0))
    high, low = split(jnp.concatenate(pieces, axis=1))
    load_t[0].wait()
    total = dot(jnp.concatenate([high, low], axis=0), TH[...])
    load_t[1].wait()
    PT[...] = total[:72] + total[72:] + dot(high, TL[...])

    for r in range(8):
        pltpu.make_async_copy(PT.at[pl.ds(4 * r, 4)], potential.at[r], sem.at[6]).start()
    pltpu.make_async_copy(D, D, sem.at[2]).wait()
    load_m.wait()
    for j in range(4):
        centre = 1.0 + ((row * 8 + 2 * j + pair_row((8, 128))).astype(F32) + 0.5) * DR
        scale = lanes((DT / (2.0 * DPHI)) / centre, NPHI)
        mine = PT[pl.ds(8 * j, 8)]
        slope = PT[pl.ds(40 + 8 * j, 8)] - PT[pl.ds(32 + 8 * j, 8)]
        around = pltpu.roll(mine, NPHI - 1, 1) - pltpu.roll(mine, 1, 1)
        OUT[0, j] = M[0, j] - (DT / (2.0 * DR)) * D[j] * slope
        OUT[1, j] = M[1, j] - scale * D[j] * around
        for i in range(2):
            for h in range(2):
                pltpu.make_async_copy(
                    OUT.at[i, j, pl.ds(4 * h, 4)], new_state.at[1 + i, 2 * j + h], sem.at[7]
                ).start()
    pltpu.make_async_copy(OUT, OUT, sem.at[7]).wait()
    pltpu.make_async_copy(PT.at[pl.ds(0, 32)], PT.at[pl.ds(0, 32)], sem.at[6]).wait()
    for i in range(2):
        pltpu.make_async_copy(M.at[0], M.at[0], sem.at[4 + i]).wait()


def body(state, green, vertical):
    f_high, f_low, i_high, i_low = (jnp.asarray(t) for t in tables())
    anywhere = pl.BlockSpec(memory_space=pl.ANY)
    vmem = pl.BlockSpec(memory_space=pltpu.VMEM)
    dma = pltpu.SemaphoreType.DMA
    pair = (8, NPHI)
    part, spec = pl.pallas_call(
        exchange_kernel,
        out_shape=(
            jax.ShapeDtypeStruct((4, 4, *pair), F32),
            jax.ShapeDtypeStruct((ROWS, 128), F32),
        ),
        in_specs=[anywhere, anywhere, vmem, anywhere, anywhere],
        out_specs=(anywhere, anywhere),
        scratch_shapes=[
            pltpu.VMEM((4, 6, *pair), F32),
            pltpu.VMEM((4, 6, *pair), F32),
            pltpu.VMEM((NPHI, 2 * MODES), BF16),
            pltpu.VMEM((NPHI, 2 * MODES), BF16),
            pltpu.VMEM((NR, NR), BF16),
            pltpu.VMEM((128, 2 * MODES), F32),
            pltpu.VMEM((ROWS, 128), F32),
            pltpu.VMEM((ROWS, 1, 128), F32),
            pltpu.VMEM((ROWS, 128), F32),
            pltpu.VMEM((ROWS, 128), F32),
            pltpu.VMEM((4, *pair), F32),
            pltpu.VMEM((4, *pair), F32),
            pltpu.VMEM((4, *pair), F32),
            pltpu.VMEM((4, 5, *pair), F32),
            pltpu.VMEM((4, 4, *pair), F32),
            dma((6,)), dma((4,)), dma((4,)), dma, dma, dma, dma, dma((2,)), dma((2,)), dma((2,)),
        ],
        compiler_params=pltpu.CompilerParams(
            collective_id=0, has_side_effects=True, vmem_limit_bytes=40 << 20
        ),
        name="exchange",
    )(state, green.reshape(NR, NR), vertical, f_high, f_low)
    return pl.pallas_call(
        finish_kernel,
        out_shape=(
            jax.ShapeDtypeStruct((4, 8, 4, NPHI), F32),
            jax.ShapeDtypeStruct((8, 4, NPHI), F32),
        ),
        in_specs=[anywhere, anywhere, vmem, anywhere, anywhere],
        out_specs=(anywhere, anywhere),
        scratch_shapes=[
            pltpu.VMEM((4, *pair), F32),
            pltpu.VMEM((2, 4, *pair), F32),
            pltpu.VMEM((2 * MODES, NPHI), BF16),
            pltpu.VMEM((2 * MODES, NPHI), BF16),
            pltpu.VMEM((72, NPHI), F32),
            pltpu.VMEM((2, 4, *pair), F32),
            dma((8,)),
        ],
        compiler_params=pltpu.CompilerParams(vmem_limit_bytes=24 << 20),
        name="finish",
    )(state, part, spec, i_high, i_low)


def solution(mesh):
    placed = (P(None, "row", "gz", None), P("row", None, None), P())
    return jax.shard_map(
        body,
        mesh=mesh,
        in_specs=placed,
        out_specs=(P(None, "row", "gz", None), P("row", "gz", None)),
        check_vma=False,
    )
```

```python
import functools
import math

import jax
import jax.numpy as jnp
import ml_dtypes
import numpy as np
from jax import lax
from jax.experimental import pallas as pl
from jax.experimental.pallas import tpu as pltpu
from jax.sharding import PartitionSpec as P

NR, NPHI, MODES, ZW = 1024, 2048, 128, 16
ROWS, GZ = 128, 4
DR = 4.0 / NR
DPHI = 2.0 * math.pi / NPHI
DT = 0.2 * min(DR, DPHI)
F32, BF16 = jnp.float32, jnp.bfloat16
MESH = pl.DeviceIdType.MESH
CHUNK = 256


def tables():
    index = np.arange(NPHI)[:, None] * np.arange(MODES)[None, :] % NPHI
    angles = 2.0 * np.pi * index / NPHI
    forward = np.concatenate([np.cos(angles), -np.sin(angles)], axis=1)
    weights = np.where(np.arange(MODES) == 0, 1.0, 2.0) / NPHI
    inverse = forward.T * np.concatenate([weights, weights])[:, None]
    out = []
    for table in (forward, inverse):
        high = table.astype(np.float32).astype(ml_dtypes.bfloat16)
        low = (table - high.astype(np.float64)).astype(np.float32).astype(ml_dtypes.bfloat16)
        out += [high, low]
    return out


def split(x):
    high = x.astype(BF16)
    return high, (x - high.astype(F32)).astype(BF16)


def dot(a, b):
    return jnp.dot(a, b, preferred_element_type=F32)


def iota(shape, dim):
    return lax.broadcasted_iota(jnp.int32, shape, dim)


def minmod_half(a, b):
    return jnp.where(a * b > 0, jnp.where(jnp.abs(a) < jnp.abs(b), a, b), 0.0) * 0.5


def rusanov(left, right, normal):
    v_left = left[normal] / left[0]
    v_right = right[normal] / right[0]
    reach = jnp.maximum(jnp.abs(v_left), jnp.abs(v_right)) + 1.0
    fluxes = []
    for k in range(4):
        both = left[k] * v_left + right[k] * v_right
        if k == normal:
            both = both + (left[0] + right[0])
        fluxes.append(0.5 * (both - reach * (right[k] - left[k])))
    return fluxes


def lanes(column, width):
    return jnp.concatenate([column] * (width // 128), axis=1)


def pair_row(shape):
    return (iota(shape, 0) >= 4).astype(jnp.int32)


def peer(row, k):
    step, low = k // 8, 7 - lax.rem(k, 8)
    half = (step + 1) // 2
    shift = jnp.where(lax.rem(step, 2) == 0, 8 + half, 8 - half)
    z, q = row // 8, lax.rem(row, 8)
    return lax.rem(z + shift, 16) * 8 + (q ^ low)


def exchange_kernel(
    state, green, vertical, t_high, t_low, part, spec,
    V, HO, HI, S, O, TH, TL, G, SA, msg, X, back, Y, LB, RB, FB, FR, acc,
    sem_in, sem_gs, sem_gr, sem_as, sem_ar, sem_bs, sem_br, sem_hs, sem_hr, sem_out,
):
    row, gz = lax.axis_index("row"), lax.axis_index("gz")

    def load_rows(fields, target, shift, sem):
        for r in range(8):
            t = r + 2 - shift
            pltpu.make_async_copy(
                state.at[fields, r], target.at[fields, t // 2, pl.ds(4 * (t % 2), 4)], sem
            ).start()

    load_rows(pl.ds(0, 1), S, 0, sem_in.at[0])
    load_t = [
        pltpu.make_async_copy(t_high, TH, sem_in.at[1]),
        pltpu.make_async_copy(t_low, TL, sem_in.at[2]),
    ]
    for copy in load_t:
        copy.start()
    load_rows(pl.ds(1, 3), S, 0, sem_in.at[3])
    load_rows(pl.ds(0, 4), O, 1, sem_in.at[4])
    load_g = pltpu.make_async_copy(green, G, sem_in.at[5])
    load_g.start()
    load_v = pltpu.make_async_copy(vertical, V, sem_in.at[6])
    load_v.start()

    barrier = pltpu.get_barrier_semaphore()

    def greet(k, carry):
        pl.semaphore_signal(barrier, inc=1, device_id=(peer(row, k), gz), device_id_type=MESH)
        return carry

    for k in range(1, GZ):
        pl.semaphore_signal(barrier, inc=1, device_id=(row, gz ^ k), device_id_type=MESH)
    lax.fori_loop(0, ROWS - 1, greet, 0)

    pltpu.make_async_copy(S.at[0, pl.ds(1, 4)], S.at[0, pl.ds(1, 4)], sem_in.at[0]).wait()
    density = S[0, pl.ds(1, 4)].reshape(32, NPHI)
    high, low = split(density)
    load_t[0].wait()
    stacked = dot(jnp.concatenate([high, low], axis=0), TH[...])
    load_t[1].wait()
    own = pl.ds(pl.multiple_of(gz * 32, 32), 32)
    SA[own, :] = stacked[:32] + stacked[32:] + dot(high, TL[...])

    pl.semaphore_wait(barrier, ROWS - 1 + GZ - 1)
    gathers = []
    for k in range(1, GZ):
        gathers.append(
            pltpu.make_async_remote_copy(
                SA.at[own], SA.at[own], sem_gs.at[k], sem_gr.at[k],
                device_id=(row, gz ^ k), device_id_type=MESH,
            )
        )
        gathers[-1].start()

    a_row, a_col = iota((256, 16), 0), iota((256, 16), 1)
    pick_y = (a_col == 4 * ((a_row >> 5) & 3) + (a_row & 3)).astype(BF16)
    b_row, b_col = iota((16, 128), 0), iota((16, 128), 1)
    pick_z = (b_row == 4 * gz + (b_col & 3)).astype(BF16)
    w_row, w_col = iota((256, 128), 0), iota((256, 128), 1)
    w_keep = ((w_row >> 7) == (w_col >> 6)) & (((w_row >> 2) & 7) == ((w_col >> 2) & 15))
    weights = []
    load_v.wait()
    for piece in split(V[...]):
        rows_y = lax.dot_general(
            pick_y, piece, (((1,), (1,)), ((), ())), preferred_element_type=F32
        ).astype(BF16)
        weights.append(jnp.where(w_keep, dot(rows_y, pick_z), 0.0).astype(BF16))
    for copy in gathers:
        copy.wait()
    turned = jnp.concatenate([SA[:, :MODES].T, SA[:, MODES:].T], axis=1)
    high, low = split(turned)
    mixed = dot(high, weights[0]) + dot(low, weights[0]) + dot(high, weights[1])
    msg[...] = mixed.astype(BF16).astype(F32)

    def send_forward(k, carry):
        d = peer(row, k)
        pltpu.make_async_remote_copy(
            msg.at[pl.ds(d, 1)], X.at[row], sem_as, sem_ar, device_id=(d, gz), device_id_type=MESH
        ).start()
        return carry

    lax.fori_loop(0, ROWS - 1, send_forward, 0)
    X[row] = msg[pl.ds(row, 1), :]

    pltpu.make_async_copy(
        S.at[pl.ds(1, 3), pl.ds(1, 4)], S.at[pl.ds(1, 3), pl.ds(1, 4)], sem_in.at[3]
    ).wait()
    pltpu.make_async_copy(O.at[:, pl.ds(0, 4)], O.at[:, pl.ds(0, 4)], sem_in.at[4]).wait()
    for side, j in ((0, 1), (1, 4)):
        HO[side] = S[:, j].reshape(32, NPHI).astype(BF16)
    down = pltpu.make_async_remote_copy(
        HO.at[0], HI.at[0], sem_hs.at[0], sem_hr.at[0],
        device_id=(jnp.maximum(row - 1, 0), gz), device_id_type=MESH,
    )
    up = pltpu.make_async_remote_copy(
        HO.at[1], HI.at[1], sem_hs.at[1], sem_hr.at[1],
        device_id=(jnp.minimum(row + 1, ROWS - 1), gz), device_id_type=MESH,
    )

    @pl.when(row > 0)
    def _():
        down.start()

    @pl.when(row < ROWS - 1)
    def _():
        up.start()

    first = row * 8

    def azimuth(j, carry):
        centre = 1.0 + ((first + 2 * j + pair_row((8, 128))).astype(F32) + 0.5) * DR
        inverse_r = lanes(1.0 / centre, CHUNK)
        for k in range(4):
            u = S[k, j + 1]
            back_diff = u - pltpu.roll(u, 1, 1)
            slope = minmod_half(back_diff, pltpu.roll(back_diff, NPHI - 1, 1))
            LB[k] = u + slope
            RB[k] = pltpu.roll(u - slope, NPHI - 1, 1)

        for c in range(NPHI // CHUNK):
            at = pl.ds(c * CHUNK, CHUNK)
            fluxes = rusanov([LB[k, :, at] for k in range(4)], [RB[k, :, at] for k in range(4)], 2)
            for k in range(4):
                FB[k, :, at] = fluxes[k]

        for k in range(4):
            flux = FB[k]
            LB[k] = flux - pltpu.roll(flux, 1, 1)

        for c in range(NPHI // CHUNK):
            at = pl.ds(c * CHUNK, CHUNK)
            u = [S[k, j + 1, :, at] for k in range(4)]
            spin = u[2] / u[0]
            acc[4, j, :, at] = DT * u[0]
            gain = [None, u[2] * spin + u[0], -(u[1] * spin), None]
            for k in range(4):
                change = LB[k, :, at] * (-1.0 / DPHI)
                if gain[k] is not None:
                    change = change + gain[k]
                acc[k, j, :, at] = u[k] + DT * inverse_r * change
        return carry

    lax.fori_loop(0, 4, azimuth, 0)

    def radial(j, c):
        at = pl.ds(pl.multiple_of(c * CHUNK, CHUNK), CHUNK)
        face = lanes(1.0 + (first + 2 * j + pair_row((8, 128))).astype(F32) * DR, CHUNK)
        left, right = [], []
        for k in range(4):
            a0, a1, a2, a3 = S[k, j, :, at], O[k, j, :, at], S[k, j + 1, :, at], O[k, j + 1, :, at]
            middle = a2 - a1
            left.append(a1 + minmod_half(a1 - a0, middle))
            right.append(a2 - minmod_half(middle, a3 - a2))
        fluxes = rusanov(left, right, 1)
        for k in range(4):
            FR[k, j, :, at] = face * fluxes[k]

    pieces = NPHI // CHUNK

    def inner(i, carry):
        radial(1 + i // pieces, lax.rem(i, pieces))
        return carry

    lax.fori_loop(0, 2 * pieces, inner, 0)

    pltpu.make_async_copy(X.at[pl.ds(0, ROWS - 1)], X.at[pl.ds(0, ROWS - 1)], sem_ar).wait()
    load_g.wait()
    sub, lane = iota((ROWS, 8, 128), 1), iota((ROWS, 8, 128), 2)
    group = (lane >> 2) & 15
    spread = jnp.where(group == sub, jnp.broadcast_to(X[...], (ROWS, 8, 128)), 0.0)
    f_row, f_col = iota((128, 128), 0), iota((128, 128), 1)
    fold = (((f_row >> 6) == (f_col >> 6)) & ((f_row & 3) == (f_col & 3))).astype(BF16)
    columns = dot(spread.reshape(NR, 128).astype(BF16), fold).astype(BF16)
    solved = dot(G[...], columns).reshape(ROWS, 8, 128)
    keep = (group == sub + 1) | ((group == 0) & (sub == 7)) | ((group == 9) & (sub == 0))
    rows = jnp.sum(jnp.where(keep, solved, 0.0), axis=1)
    f_group = (f_col >> 2) & 15
    back[...] = jnp.where(
        f_group == 0, pltpu.roll(rows, 1, 0),
        jnp.where(f_group == 9, pltpu.roll(rows, ROWS - 1, 0), rows),
    )

    def send_back(k, carry):
        d = peer(row, k)
        pltpu.make_async_remote_copy(
            back.at[pl.ds(d, 1)], Y.at[pl.ds(row, 1)], sem_bs, sem_br,
            device_id=(d, gz), device_id_type=MESH,
        ).start()
        return carry

    lax.fori_loop(0, ROWS - 1, send_back, 0)
    Y[pl.ds(row, 1), :] = back[pl.ds(row, 1), :]

    @pl.when(row > 0)
    def _():
        down.wait_send()
        up.wait_recv()

    @pl.when(row < ROWS - 1)
    def _():
        up.wait_send()
        down.wait_recv()

    @pl.when(row > 0)
    def _():
        S[:, 0] = HI[1].astype(F32).reshape(4, 8, NPHI)

    @pl.when(row < ROWS - 1)
    def _():
        S[:, 5] = HI[0].astype(F32).reshape(4, 8, NPHI)

    @pl.when(row == 0)
    def _():
        for k in range(4):
            S[k, 0, pl.ds(0, 4)] = S[k, 1, pl.ds(0, 4)]
            S[k, 0, pl.ds(4, 4)] = S[k, 1, pl.ds(0, 4)]

    @pl.when(row == ROWS - 1)
    def _():
        for k in range(4):
            S[k, 5, pl.ds(0, 4)] = S[k, 4, pl.ds(4, 4)]
            S[k, 5, pl.ds(4, 4)] = S[k, 4, pl.ds(4, 4)]

    for k in range(4):
        O[k, 0, pl.ds(0, 4)] = S[k, 0, pl.ds(4, 4)]
        O[k, 4, pl.ds(4, 4)] = S[k, 5, pl.ds(0, 4)]
        O[k, 5, pl.ds(0, 4)] = S[k, 5, pl.ds(4, 4)]
        O[k, 5, pl.ds(4, 4)] = S[k, 5, pl.ds(4, 4)]

    def edges(i, carry):
        piece = lax.rem(i, pieces)
        which = i // pieces
        radial(jnp.where(which == 0, 0, which + 2), piece)
        return carry

    lax.fori_loop(0, 3 * pieces, edges, 0)

    def gather_radial(i, carry):
        j, c = i // pieces, lax.rem(i, pieces)
        at = pl.ds(pl.multiple_of(c * CHUNK, CHUNK), CHUNK)
        centre = 1.0 + ((first + 2 * j + pair_row((8, 128))).astype(F32) + 0.5) * DR
        scale = lanes((DT / DR) / centre, CHUNK)
        second = iota((8, CHUNK), 0) >= 4
        for k in range(4):
            low_face = FR[k, j, :, at]
            high_face = pltpu.roll(jnp.where(second, low_face, FR[k, j + 1, :, at]), 4, 0)
            acc[k, j, :, at] = acc[k, j, :, at] - scale * (high_face - low_face)
        return carry

    lax.fori_loop(0, 4 * pieces, gather_radial, 0)
    out_part = pltpu.make_async_copy(acc, part, sem_out.at[0])
    out_part.start()

    pltpu.make_async_copy(Y.at[pl.ds(0, ROWS - 1)], Y.at[pl.ds(0, ROWS - 1)], sem_br).wait()
    out_spec = pltpu.make_async_copy(Y, spec, sem_out.at[1])
    out_spec.start()
    pltpu.make_async_copy(X.at[pl.ds(0, ROWS - 1)], X.at[pl.ds(0, ROWS - 1)], sem_as).wait()
    pltpu.make_async_copy(Y.at[pl.ds(0, ROWS - 1)], Y.at[pl.ds(0, ROWS - 1)], sem_bs).wait()
    out_part.wait()
    out_spec.wait()


def finish_kernel(part, spec, t_high, t_low, new_state, potential, Y, D, M, TH, TL, PT, OUT, sem):
    row = lax.axis_index("row")
    load_y = pltpu.make_async_copy(spec, Y, sem.at[8])
    load_y.start()
    load_t = [
        pltpu.make_async_copy(t_high, TH, sem.at[0]),
        pltpu.make_async_copy(t_low, TL, sem.at[1]),
    ]
    for copy in load_t:
        copy.start()
    load_d = pltpu.make_async_copy(part.at[4], D, sem.at[2])
    load_d.start()
    load_m = pltpu.make_async_copy(part.at[pl.ds(1, 2)], M, sem.at[3])
    load_m.start()
    plain = []
    for i, k in enumerate((0, 3)):
        for r in range(8):
            plain.append(
                pltpu.make_async_copy(
                    part.at[k, r // 2, pl.ds(4 * (r % 2), 4)], new_state.at[k, r], sem.at[4 + i]
                )
            )
            plain[-1].start()

    load_y.wait()
    turned = Y[...].T
    pieces = []
    for c in range(2):
        base = 64 * c
        own = turned[base + 4 : base + 36]
        ext = turned[base : base + 40]
        before = jnp.where(row == 0, turned[base + 4 : base + 8], turned[base : base + 4])
        after = jnp.where(row == ROWS - 1, turned[base + 32 : base + 36], turned[base + 36 : base + 40])
        pieces.append(jnp.concatenate([own, before, ext[4:36], after], axis=0))
    high, low = split(jnp.concatenate(pieces, axis=1))
    load_t[0].wait()
    total = dot(jnp.concatenate([high, low], axis=0), TH[...])
    load_t[1].wait()
    PT[...] = total[:72] + total[72:] + dot(high, TL[...])

    for r in range(8):
        pltpu.make_async_copy(PT.at[pl.ds(4 * r, 4)], potential.at[r], sem.at[6]).start()
    load_d.wait()
    load_m.wait()
    for j in range(4):
        centre = 1.0 + ((row * 8 + 2 * j + pair_row((8, 128))).astype(F32) + 0.5) * DR
        scale = lanes((1.0 / (2.0 * DPHI)) / centre, NPHI)
        mine = PT[pl.ds(8 * j, 8)]
        slope = PT[pl.ds(40 + 8 * j, 8)] - PT[pl.ds(32 + 8 * j, 8)]
        around = pltpu.roll(mine, NPHI - 1, 1) - pltpu.roll(mine, 1, 1)
        OUT[0, j] = M[0, j] - (1.0 / (2.0 * DR)) * D[j] * slope
        OUT[1, j] = M[1, j] - scale * D[j] * around
        for i in range(2):
            for h in range(2):
                pltpu.make_async_copy(
                    OUT.at[i, j, pl.ds(4 * h, 4)], new_state.at[1 + i, 2 * j + h], sem.at[7]
                ).start()
    pltpu.make_async_copy(OUT, OUT, sem.at[7]).wait()
    pltpu.make_async_copy(PT.at[pl.ds(0, 32)], PT.at[pl.ds(0, 32)], sem.at[6]).wait()
    for i in range(2):
        pltpu.make_async_copy(M.at[0], M.at[0], sem.at[4 + i]).wait()


def body(state, green, vertical):
    f_high, f_low, i_high, i_low = (jnp.asarray(t) for t in tables())
    anywhere = pl.BlockSpec(memory_space=pl.ANY)
    dma = pltpu.SemaphoreType.DMA
    pair = (8, NPHI)
    part, spec = pl.pallas_call(
        exchange_kernel,
        out_shape=(
            jax.ShapeDtypeStruct((5, 4, *pair), F32),
            jax.ShapeDtypeStruct((ROWS, 128), F32),
        ),
        in_specs=[anywhere] * 5,
        out_specs=(anywhere, anywhere),
        scratch_shapes=[
            pltpu.VMEM((ZW, ZW), F32),
            pltpu.VMEM((2, 32, NPHI), BF16),
            pltpu.VMEM((2, 32, NPHI), BF16),
            pltpu.VMEM((4, 6, *pair), F32),
            pltpu.VMEM((4, 6, *pair), F32),
            pltpu.VMEM((NPHI, 2 * MODES), BF16),
            pltpu.VMEM((NPHI, 2 * MODES), BF16),
            pltpu.VMEM((NR, NR), BF16),
            pltpu.VMEM((128, 2 * MODES), F32),
            pltpu.VMEM((ROWS, 128), F32),
            pltpu.VMEM((ROWS, 1, 128), F32),
            pltpu.VMEM((ROWS, 128), F32),
            pltpu.VMEM((ROWS, 128), F32),
            pltpu.VMEM((4, *pair), F32),
            pltpu.VMEM((4, *pair), F32),
            pltpu.VMEM((4, *pair), F32),
            pltpu.VMEM((4, 5, *pair), F32),
            pltpu.VMEM((5, 4, *pair), F32),
            dma((7,)), dma((4,)), dma((4,)), dma, dma, dma, dma, dma((2,)), dma((2,)), dma((2,)),
        ],
        compiler_params=pltpu.CompilerParams(
            collective_id=0, has_side_effects=True, vmem_limit_bytes=60 << 20
        ),
        name="exchange",
    )(state, green.reshape(NR, NR), vertical, f_high, f_low)
    return pl.pallas_call(
        finish_kernel,
        out_shape=(
            jax.ShapeDtypeStruct((4, 8, 4, NPHI), F32),
            jax.ShapeDtypeStruct((8, 4, NPHI), F32),
        ),
        in_specs=[anywhere] * 4,
        out_specs=(anywhere, anywhere),
        scratch_shapes=[
            pltpu.VMEM((ROWS, 128), F32),
            pltpu.VMEM((4, *pair), F32),
            pltpu.VMEM((2, 4, *pair), F32),
            pltpu.VMEM((2 * MODES, NPHI), BF16),
            pltpu.VMEM((2 * MODES, NPHI), BF16),
            pltpu.VMEM((72, NPHI), F32),
            pltpu.VMEM((2, 4, *pair), F32),
            dma((9,)),
        ],
        compiler_params=pltpu.CompilerParams(vmem_limit_bytes=60 << 20),
        name="finish",
    )(part, spec, i_high, i_low)


def solution(mesh):
    placed = (P(None, "row", "gz", None), P("row", None, None), P())
    return jax.shard_map(
        body,
        mesh=mesh,
        in_specs=placed,
        out_specs=(P(None, "row", "gz", None), P("row", "gz", None)),
        check_vma=False,
    )
```

```python
import functools
import math

import jax
import jax.numpy as jnp
import ml_dtypes
import numpy as np
from jax import lax
from jax.experimental import pallas as pl
from jax.experimental.pallas import tpu as pltpu
from jax.sharding import PartitionSpec as P

NR, NPHI, MODES, ZW = 1024, 2048, 128, 16
ROWS, GZ = 128, 4
DR = 4.0 / NR
DPHI = 2.0 * math.pi / NPHI
DT = 0.2 * min(DR, DPHI)
F32, BF16 = jnp.float32, jnp.bfloat16
MESH = pl.DeviceIdType.MESH
CHUNK = 256


def tables():
    index = np.arange(NPHI)[:, None] * np.arange(MODES)[None, :] % NPHI
    angles = 2.0 * np.pi * index / NPHI
    forward = np.concatenate([np.cos(angles), -np.sin(angles)], axis=1)
    weights = np.where(np.arange(MODES) == 0, 1.0, 2.0) / NPHI
    inverse = forward.T * np.concatenate([weights, weights])[:, None]
    out = []
    for table in (forward, inverse):
        high = table.astype(np.float32).astype(ml_dtypes.bfloat16)
        low = (table - high.astype(np.float64)).astype(np.float32).astype(ml_dtypes.bfloat16)
        out += [high, low]
    return out


def split(x):
    high = x.astype(BF16)
    return high, (x - high.astype(F32)).astype(BF16)


def dot(a, b):
    return jnp.dot(a, b, preferred_element_type=F32)


def iota(shape, dim):
    return lax.broadcasted_iota(jnp.int32, shape, dim)


def minmod_half(a, b):
    return jnp.where(a * b > 0, jnp.where(jnp.abs(a) < jnp.abs(b), a, b), 0.0) * 0.5


def rusanov(left, right, normal):
    v_left = left[normal] / left[0]
    v_right = right[normal] / right[0]
    reach = jnp.maximum(jnp.abs(v_left), jnp.abs(v_right)) + 1.0
    fluxes = []
    for k in range(4):
        both = left[k] * v_left + right[k] * v_right
        if k == normal:
            both = both + (left[0] + right[0])
        fluxes.append(0.5 * (both - reach * (right[k] - left[k])))
    return fluxes


def lanes(column, width):
    return jnp.concatenate([column] * (width // 128), axis=1)


def pair_row(shape):
    return (iota(shape, 0) >= 4).astype(jnp.int32)


def peer(row, k):
    step, low = k // 8, 7 - lax.rem(k, 8)
    half = (step + 1) // 2
    shift = jnp.where(lax.rem(step, 2) == 0, 8 + half, 8 - half)
    z, q = row // 8, lax.rem(row, 8)
    return lax.rem(z + shift, 16) * 8 + (q ^ low)


def exchange_kernel(
    state, green, vertical, t_high, t_low, part, spec,
    V, HO, HI, S, O, TH, TL, G, SA, msg, X, back, Y, LB, RB, FB, FR, acc,
    sem_in, sem_gs, sem_gr, sem_as, sem_ar, sem_bs, sem_br, sem_hs, sem_hr, sem_out,
):
    row, gz = lax.axis_index("row"), lax.axis_index("gz")

    def load_rows(fields, target, shift, sem):
        for r in range(8):
            t = r + 2 - shift
            pltpu.make_async_copy(
                state.at[fields, r], target.at[fields, t // 2, pl.ds(4 * (t % 2), 4)], sem
            ).start()

    load_rows(pl.ds(0, 1), S, 0, sem_in.at[0])
    load_t = [
        pltpu.make_async_copy(t_high, TH, sem_in.at[1]),
        pltpu.make_async_copy(t_low, TL, sem_in.at[2]),
    ]
    for copy in load_t:
        copy.start()
    load_rows(pl.ds(1, 3), S, 0, sem_in.at[3])
    load_rows(pl.ds(0, 4), O, 1, sem_in.at[4])
    load_g = pltpu.make_async_copy(green, G, sem_in.at[5])
    load_g.start()
    load_v = pltpu.make_async_copy(vertical, V, sem_in.at[6])
    load_v.start()

    barrier = pltpu.get_barrier_semaphore()

    def greet(k, carry):
        pl.semaphore_signal(barrier, inc=1, device_id=(peer(row, k), gz), device_id_type=MESH)
        return carry

    for k in range(1, GZ):
        pl.semaphore_signal(barrier, inc=1, device_id=(row, gz ^ k), device_id_type=MESH)
    lax.fori_loop(0, ROWS - 1, greet, 0)

    pltpu.make_async_copy(S.at[0, pl.ds(1, 4)], S.at[0, pl.ds(1, 4)], sem_in.at[0]).wait()
    density = S[0, pl.ds(1, 4)].reshape(32, NPHI)
    high, low = split(density)
    load_t[0].wait()
    stacked = dot(jnp.concatenate([high, low], axis=0), TH[...])
    load_t[1].wait()
    own = pl.ds(pl.multiple_of(gz * 32, 32), 32)
    SA[own, :] = stacked[:32] + stacked[32:] + dot(high, TL[...])

    pl.semaphore_wait(barrier, ROWS - 1 + GZ - 1)
    gathers = []
    for k in range(1, GZ):
        gathers.append(
            pltpu.make_async_remote_copy(
                SA.at[own], SA.at[own], sem_gs.at[k], sem_gr.at[k],
                device_id=(row, gz ^ k), device_id_type=MESH,
            )
        )
        gathers[-1].start()

    a_row, a_col = iota((256, 16), 0), iota((256, 16), 1)
    pick_y = (a_col == 4 * ((a_row >> 5) & 3) + (a_row & 3)).astype(BF16)
    b_row, b_col = iota((16, 128), 0), iota((16, 128), 1)
    pick_z = (b_row == 4 * gz + (b_col & 3)).astype(BF16)
    w_row, w_col = iota((256, 128), 0), iota((256, 128), 1)
    w_keep = ((w_row >> 7) == (w_col >> 6)) & (((w_row >> 2) & 7) == ((w_col >> 2) & 15))
    weights = []
    load_v.wait()
    for piece in split(V[...]):
        rows_y = lax.dot_general(
            pick_y, piece, (((1,), (1,)), ((), ())), preferred_element_type=F32
        ).astype(BF16)
        weights.append(jnp.where(w_keep, dot(rows_y, pick_z), 0.0).astype(BF16))
    for copy in gathers:
        copy.wait()
    turned = jnp.concatenate([SA[:, :MODES].T, SA[:, MODES:].T], axis=1)
    high, low = split(turned)
    mixed = dot(high, weights[0]) + dot(low, weights[0]) + dot(high, weights[1])
    msg[...] = mixed.astype(BF16).astype(F32)

    def send_forward(k, carry):
        d = peer(row, k)
        pltpu.make_async_remote_copy(
            msg.at[pl.ds(d, 1)], X.at[row], sem_as, sem_ar, device_id=(d, gz), device_id_type=MESH
        ).start()
        return carry

    lax.fori_loop(0, ROWS - 1, send_forward, 0)
    X[row] = msg[pl.ds(row, 1), :]

    pltpu.make_async_copy(
        S.at[pl.ds(1, 3), pl.ds(1, 4)], S.at[pl.ds(1, 3), pl.ds(1, 4)], sem_in.at[3]
    ).wait()
    pltpu.make_async_copy(O.at[:, pl.ds(0, 4)], O.at[:, pl.ds(0, 4)], sem_in.at[4]).wait()
    for side, j in ((0, 1), (1, 4)):
        HO[side] = S[:, j].reshape(32, NPHI).astype(BF16)
    down = pltpu.make_async_remote_copy(
        HO.at[0], HI.at[0], sem_hs.at[0], sem_hr.at[0],
        device_id=(jnp.maximum(row - 1, 0), gz), device_id_type=MESH,
    )
    up = pltpu.make_async_remote_copy(
        HO.at[1], HI.at[1], sem_hs.at[1], sem_hr.at[1],
        device_id=(jnp.minimum(row + 1, ROWS - 1), gz), device_id_type=MESH,
    )

    @pl.when(row > 0)
    def _():
        down.start()

    @pl.when(row < ROWS - 1)
    def _():
        up.start()

    first = row * 8

    def azimuth(j, carry):
        centre = 1.0 + ((first + 2 * j + pair_row((8, 128))).astype(F32) + 0.5) * DR
        inverse_r = lanes(1.0 / centre, CHUNK)
        for k in range(4):
            u = S[k, j + 1]
            back_diff = u - pltpu.roll(u, 1, 1)
            slope = minmod_half(back_diff, pltpu.roll(back_diff, NPHI - 1, 1))
            LB[k] = u + slope
            RB[k] = pltpu.roll(u - slope, NPHI - 1, 1)

        for c in range(NPHI // CHUNK):
            at = pl.ds(c * CHUNK, CHUNK)
            fluxes = rusanov([LB[k, :, at] for k in range(4)], [RB[k, :, at] for k in range(4)], 2)
            for k in range(4):
                FB[k, :, at] = fluxes[k]

        for k in range(4):
            flux = FB[k]
            LB[k] = flux - pltpu.roll(flux, 1, 1)

        for c in range(NPHI // CHUNK):
            at = pl.ds(c * CHUNK, CHUNK)
            u = [S[k, j + 1, :, at] for k in range(4)]
            spin = u[2] / u[0]
            acc[4, j, :, at] = DT * u[0]
            gain = [None, u[2] * spin + u[0], -(u[1] * spin), None]
            for k in range(4):
                change = LB[k, :, at] * (-1.0 / DPHI)
                if gain[k] is not None:
                    change = change + gain[k]
                acc[k, j, :, at] = u[k] + DT * inverse_r * change
        return carry

    lax.fori_loop(0, 4, azimuth, 0)

    def radial(j, c):
        at = pl.ds(pl.multiple_of(c * CHUNK, CHUNK), CHUNK)
        face = lanes(1.0 + (first + 2 * j + pair_row((8, 128))).astype(F32) * DR, CHUNK)
        left, right = [], []
        for k in range(4):
            a0, a1, a2, a3 = S[k, j, :, at], O[k, j, :, at], S[k, j + 1, :, at], O[k, j + 1, :, at]
            middle = a2 - a1
            left.append(a1 + minmod_half(a1 - a0, middle))
            right.append(a2 - minmod_half(middle, a3 - a2))
        fluxes = rusanov(left, right, 1)
        for k in range(4):
            FR[k, j, :, at] = face * fluxes[k]

    pieces = NPHI // CHUNK

    def inner(i, carry):
        radial(1 + i // pieces, lax.rem(i, pieces))
        return carry

    lax.fori_loop(0, 2 * pieces, inner, 0)

    pltpu.make_async_copy(X.at[pl.ds(0, ROWS - 1)], X.at[pl.ds(0, ROWS - 1)], sem_ar).wait()
    load_g.wait()
    sub, lane = iota((ROWS, 8, 128), 1), iota((ROWS, 8, 128), 2)
    group = (lane >> 2) & 15
    spread = jnp.where(group == sub, jnp.broadcast_to(X[...], (ROWS, 8, 128)), 0.0)
    f_row, f_col = iota((128, 128), 0), iota((128, 128), 1)
    fold = (((f_row >> 6) == (f_col >> 6)) & ((f_row & 3) == (f_col & 3))).astype(BF16)
    columns = dot(spread.reshape(NR, 128).astype(BF16), fold).astype(BF16)
    solved = dot(G[...], columns).reshape(ROWS, 8, 128)
    keep = (group == sub + 1) | ((group == 0) & (sub == 7)) | ((group == 9) & (sub == 0))
    rows = jnp.sum(jnp.where(keep, solved, 0.0), axis=1)
    f_group = (f_col >> 2) & 15
    back[...] = jnp.where(
        f_group == 0, pltpu.roll(rows, 1, 0),
        jnp.where(f_group == 9, pltpu.roll(rows, ROWS - 1, 0), rows),
    )

    def send_back(k, carry):
        d = peer(row, k)
        pltpu.make_async_remote_copy(
            back.at[pl.ds(d, 1)], Y.at[pl.ds(row, 1)], sem_bs, sem_br,
            device_id=(d, gz), device_id_type=MESH,
        ).start()
        return carry

    lax.fori_loop(0, ROWS - 1, send_back, 0)
    Y[pl.ds(row, 1), :] = back[pl.ds(row, 1), :]

    @pl.when(row > 0)
    def _():
        down.wait_send()
        up.wait_recv()

    @pl.when(row < ROWS - 1)
    def _():
        up.wait_send()
        down.wait_recv()

    @pl.when(row > 0)
    def _():
        S[:, 0] = HI[1].astype(F32).reshape(4, 8, NPHI)

    @pl.when(row < ROWS - 1)
    def _():
        S[:, 5] = HI[0].astype(F32).reshape(4, 8, NPHI)

    @pl.when(row == 0)
    def _():
        for k in range(4):
            S[k, 0, pl.ds(0, 4)] = S[k, 1, pl.ds(0, 4)]
            S[k, 0, pl.ds(4, 4)] = S[k, 1, pl.ds(0, 4)]

    @pl.when(row == ROWS - 1)
    def _():
        for k in range(4):
            S[k, 5, pl.ds(0, 4)] = S[k, 4, pl.ds(4, 4)]
            S[k, 5, pl.ds(4, 4)] = S[k, 4, pl.ds(4, 4)]

    for k in range(4):
        O[k, 0, pl.ds(0, 4)] = S[k, 0, pl.ds(4, 4)]
        O[k, 4, pl.ds(4, 4)] = S[k, 5, pl.ds(0, 4)]
        O[k, 5, pl.ds(0, 4)] = S[k, 5, pl.ds(4, 4)]
        O[k, 5, pl.ds(4, 4)] = S[k, 5, pl.ds(4, 4)]

    def edges(i, carry):
        piece = lax.rem(i, pieces)
        which = i // pieces
        radial(jnp.where(which == 0, 0, which + 2), piece)
        return carry

    lax.fori_loop(0, 3 * pieces, edges, 0)

    def gather_radial(i, carry):
        j, c = i // pieces, lax.rem(i, pieces)
        at = pl.ds(pl.multiple_of(c * CHUNK, CHUNK), CHUNK)
        centre = 1.0 + ((first + 2 * j + pair_row((8, 128))).astype(F32) + 0.5) * DR
        scale = lanes((DT / DR) / centre, CHUNK)
        second = iota((8, CHUNK), 0) >= 4
        for k in range(4):
            low_face = FR[k, j, :, at]
            high_face = pltpu.roll(jnp.where(second, low_face, FR[k, j + 1, :, at]), 4, 0)
            acc[k, j, :, at] = acc[k, j, :, at] - scale * (high_face - low_face)
        return carry

    lax.fori_loop(0, 4 * pieces, gather_radial, 0)
    out_part = pltpu.make_async_copy(acc, part, sem_out.at[0])
    out_part.start()

    pltpu.make_async_copy(Y.at[pl.ds(0, ROWS - 1)], Y.at[pl.ds(0, ROWS - 1)], sem_br).wait()
    out_spec = pltpu.make_async_copy(Y, spec, sem_out.at[1])
    out_spec.start()
    pltpu.make_async_copy(X.at[pl.ds(0, ROWS - 1)], X.at[pl.ds(0, ROWS - 1)], sem_as).wait()
    pltpu.make_async_copy(Y.at[pl.ds(0, ROWS - 1)], Y.at[pl.ds(0, ROWS - 1)], sem_bs).wait()
    out_part.wait()
    out_spec.wait()


def finish_kernel(part, spec, t_high, t_low, new_state, potential, Y, D, M, N, TH, TL, PT, OUT, sem):
    row = lax.axis_index("row")
    load_y = pltpu.make_async_copy(spec, Y, sem.at[8])
    load_y.start()
    load_t = [
        pltpu.make_async_copy(t_high, TH, sem.at[0]),
        pltpu.make_async_copy(t_low, TL, sem.at[1]),
    ]
    for copy in load_t:
        copy.start()
    load_d = pltpu.make_async_copy(part.at[4], D, sem.at[2])
    load_d.start()
    load_m = pltpu.make_async_copy(part.at[pl.ds(1, 2)], M, sem.at[3])
    load_m.start()
    load_n = []
    for i, k in enumerate((0, 3)):
        load_n.append(pltpu.make_async_copy(part.at[k], N.at[i], sem.at[4 + i]))
        load_n[-1].start()

    load_y.wait()
    turned = Y[...].T
    pieces = []
    for c in range(2):
        base = 64 * c
        own = turned[base + 4 : base + 36]
        ext = turned[base : base + 40]
        before = jnp.where(row == 0, turned[base + 4 : base + 8], turned[base : base + 4])
        after = jnp.where(row == ROWS - 1, turned[base + 32 : base + 36], turned[base + 36 : base + 40])
        pieces.append(jnp.concatenate([own, before, ext[4:36], after], axis=0))
    high, low = split(jnp.concatenate(pieces, axis=1))
    load_t[0].wait()
    total = dot(jnp.concatenate([high, low], axis=0), TH[...])
    load_t[1].wait()
    PT[...] = total[:72] + total[72:] + dot(high, TL[...])

    for r in range(8):
        pltpu.make_async_copy(PT.at[pl.ds(4 * r, 4)], potential.at[r], sem.at[6]).start()
    for i, k in enumerate((0, 3)):
        load_n[i].wait()
        for r in range(8):
            pltpu.make_async_copy(
                N.at[i, r // 2, pl.ds(4 * (r % 2), 4)], new_state.at[k, r], sem.at[9 + i]
            ).start()
    load_d.wait()
    load_m.wait()
    for j in range(4):
        centre = 1.0 + ((row * 8 + 2 * j + pair_row((8, 128))).astype(F32) + 0.5) * DR
        scale = lanes((1.0 / (2.0 * DPHI)) / centre, NPHI)
        mine = PT[pl.ds(8 * j, 8)]
        slope = PT[pl.ds(40 + 8 * j, 8)] - PT[pl.ds(32 + 8 * j, 8)]
        around = pltpu.roll(mine, NPHI - 1, 1) - pltpu.roll(mine, 1, 1)
        OUT[0, j] = M[0, j] - (1.0 / (2.0 * DR)) * D[j] * slope
        OUT[1, j] = M[1, j] - scale * D[j] * around
        for i in range(2):
            for h in range(2):
                pltpu.make_async_copy(
                    OUT.at[i, j, pl.ds(4 * h, 4)], new_state.at[1 + i, 2 * j + h], sem.at[7]
                ).start()
    pltpu.make_async_copy(OUT, OUT, sem.at[7]).wait()
    pltpu.make_async_copy(PT.at[pl.ds(0, 32)], PT.at[pl.ds(0, 32)], sem.at[6]).wait()
    for i in range(2):
        pltpu.make_async_copy(N.at[i], N.at[i], sem.at[9 + i]).wait()


def body(state, green, vertical):
    f_high, f_low, i_high, i_low = (jnp.asarray(t) for t in tables())
    anywhere = pl.BlockSpec(memory_space=pl.ANY)
    dma = pltpu.SemaphoreType.DMA
    pair = (8, NPHI)
    part, spec = pl.pallas_call(
        exchange_kernel,
        out_shape=(
            jax.ShapeDtypeStruct((5, 4, *pair), F32),
            jax.ShapeDtypeStruct((ROWS, 128), F32),
        ),
        in_specs=[anywhere] * 5,
        out_specs=(anywhere, anywhere),
        scratch_shapes=[
            pltpu.VMEM((ZW, ZW), F32),
            pltpu.VMEM((2, 32, NPHI), BF16),
            pltpu.VMEM((2, 32, NPHI), BF16),
            pltpu.VMEM((4, 6, *pair), F32),
            pltpu.VMEM((4, 6, *pair), F32),
            pltpu.VMEM((NPHI, 2 * MODES), BF16),
            pltpu.VMEM((NPHI, 2 * MODES), BF16),
            pltpu.VMEM((NR, NR), BF16),
            pltpu.VMEM((128, 2 * MODES), F32),
            pltpu.VMEM((ROWS, 128), F32),
            pltpu.VMEM((ROWS, 1, 128), F32),
            pltpu.VMEM((ROWS, 128), F32),
            pltpu.VMEM((ROWS, 128), F32),
            pltpu.VMEM((4, *pair), F32),
            pltpu.VMEM((4, *pair), F32),
            pltpu.VMEM((4, *pair), F32),
            pltpu.VMEM((4, 5, *pair), F32),
            pltpu.VMEM((5, 4, *pair), F32),
            dma((7,)), dma((4,)), dma((4,)), dma, dma, dma, dma, dma((2,)), dma((2,)), dma((2,)),
        ],
        compiler_params=pltpu.CompilerParams(
            collective_id=0, has_side_effects=True, vmem_limit_bytes=60 << 20
        ),
        name="exchange",
    )(state, green.reshape(NR, NR), vertical, f_high, f_low)
    return pl.pallas_call(
        finish_kernel,
        out_shape=(
            jax.ShapeDtypeStruct((4, 8, 4, NPHI), F32),
            jax.ShapeDtypeStruct((8, 4, NPHI), F32),
        ),
        in_specs=[anywhere] * 4,
        out_specs=(anywhere, anywhere),
        scratch_shapes=[
            pltpu.VMEM((ROWS, 128), F32),
            pltpu.VMEM((4, *pair), F32),
            pltpu.VMEM((2, 4, *pair), F32),
            pltpu.VMEM((2, 4, *pair), F32),
            pltpu.VMEM((2 * MODES, NPHI), BF16),
            pltpu.VMEM((2 * MODES, NPHI), BF16),
            pltpu.VMEM((72, NPHI), F32),
            pltpu.VMEM((2, 4, *pair), F32),
            dma((11,)),
        ],
        compiler_params=pltpu.CompilerParams(vmem_limit_bytes=60 << 20),
        name="finish",
    )(part, spec, i_high, i_low)


def solution(mesh):
    placed = (P(None, "row", "gz", None), P("row", None, None), P())
    return jax.shard_map(
        body,
        mesh=mesh,
        in_specs=placed,
        out_specs=(P(None, "row", "gz", None), P("row", "gz", None)),
        check_vma=False,
    )
```
